32 devices in a mesh: dom: 8 (over z, y), rep: 4 (over x, core).
Axes of the slice: x: 2, y: 2, z: 4, core: 2. Of those that a mesh axis runs over, the one named last changes fastest.
Arguments:
- x_loader: bfloat16 [16384, 512], P(('dom', 'rep')), may hold values from -6 to 6
- owner_index: int32 [16384], P(('dom', 'rep')), may hold values from 0 to 16383, as said below
- tile_vals: bfloat16 [128, 12, 128, 128], P(('dom', 'rep')), as said below
- tile_cols: int32 [128, 12], P(('dom', 'rep')), may hold values from 0 to 127, as said below
- tile_live: int32 [128, 12], P(('dom', 'rep')), may hold values from 0 to 1, as said below
- w_self: bfloat16 [512, 512], replicated, may hold values from -0.25 to 0.25
- w_neigh: bfloat16 [512, 512], replicated, may hold values from -3 to 3
- bias: float32 [512], replicated, may hold values from -3 to 3
- cotangent: bfloat16 [16384, 512], P(('dom', 'rep')), may hold values from -6 to 6
Outputs:
- layer_out: bfloat16 [16384, 512], P(('dom', 'rep'))
- grad_features: bfloat16 [16384, 512], P(('dom', 'rep'))
- grad_self: float32 [512, 512], replicated
- grad_neigh: float32 [512, 512], replicated
- grad_bias: float32 [512], replicated
The draws below stay inside these ranges and needn't reach their ends.
Inputs may be any that keep to these rules, and one draw needn't show every extreme that they name: `owner_index`: A permutation of the 16384 rows. Loader rows are in blocks of 512 in the order of the devices (dom slowest); owner rows likewise. The 512 rows of each loader block with rep index r go to owner blocks of rep index r, 64 rows to each of the 8 partitions. `tile_cols`: partition p holds row tiles p * 16 to (p + 1) * 16 - 1. A column tile of a row tile of partition p lies in partition p or within 4 tiles beyond its edges. W is symmetric: every live slot (t, c) with tiles B is matched by a live slot (c, t) with tiles B^T, a slot with c = t holding a symmetric tile. `tile_live`: live slots are symmetric as stated for tile_cols. `tile_vals`: nonnegative edge weights.
All inputs are finite; a program needn't handle non-finite values.
Results may differ from the reference program's by a relative error of at most 0.0075.
Values may be sent and summed in bfloat16 or wider, within the bound.
A program may use at most 64 MiB of HBM per device.

```python
import jax
import jax.numpy as jnp
from jax import lax

F = 512
RD = 512
K = 12
HALO_T = 4
NPART = 8
REPS = 4
PT = 16
V = 16384
NT = 128
SENDS = 64


def permute_many(key, count, length):
    return jax.vmap(lambda sub: jax.random.permutation(sub, length))(jax.random.split(key, count))


def draw_owner_index(key, part):
    first_key = jax.random.fold_in(key, 11)
    second_key = jax.random.fold_in(key, 12)
    slot_perm = permute_many(first_key, REPS * NPART, RD).reshape(REPS, NPART, NPART, SENDS)
    slot_grid = jnp.transpose(slot_perm, (0, 2, 1, 3))
    dest_part = jnp.arange(NPART, dtype=jnp.int32)[None, None, :, None]
    rep_ids = jnp.arange(REPS, dtype=jnp.int32)[:, None, None, None]
    owner = dest_part * (RD * REPS) + rep_ids * RD + slot_grid.astype(jnp.int32)
    owner = owner.reshape(REPS, NPART, RD)
    shuffle = permute_many(second_key, REPS * NPART, RD).reshape(REPS, NPART, RD)
    owner = jnp.take_along_axis(owner, shuffle, axis=2)
    return jnp.transpose(owner, (1, 0, 2)).reshape(NPART * REPS * RD).astype(jnp.int32)


def intra_partners(key):
    perms = permute_many(key, NPART, PT).astype(jnp.int32)
    inverse = jnp.argsort(perms, axis=1).astype(jnp.int32)
    partner_pos = jnp.take_along_axis(perms, inverse ^ 1, axis=1)
    return (jnp.arange(NPART, dtype=jnp.int32)[:, None] * PT + partner_pos).reshape(NT)


def cross_partners(key):
    border = permute_many(jax.random.fold_in(key, 1), NPART, HALO_T).astype(jnp.int32)
    border_inv = jnp.argsort(border, axis=1).astype(jnp.int32)
    middle_len = PT - 2 * HALO_T
    middle = permute_many(jax.random.fold_in(key, 2), NPART, middle_len).astype(jnp.int32)
    middle_inv = jnp.argsort(middle, axis=1).astype(jnp.int32)
    pos = jnp.arange(PT, dtype=jnp.int32)
    parts = jnp.arange(NPART, dtype=jnp.int32)[:, None]
    own = parts * PT + pos[None, :]
    last_a = jnp.clip(pos - (PT - HALO_T), 0, HALO_T - 1)
    upper = (parts + 1) * PT + border[:, last_a]
    upper = jnp.where(parts == NPART - 1, own, upper)
    first_c = jnp.clip(pos, 0, HALO_T - 1)
    prev_inv = jnp.roll(border_inv, 1, axis=0)
    lower = (parts - 1) * PT + (PT - HALO_T) + prev_inv[:, first_c]
    lower = jnp.where(parts == 0, own, lower)
    mid_m = jnp.clip(pos - HALO_T, 0, middle_len - 1)
    mid_rank = jnp.broadcast_to(middle_inv[:, mid_m], (NPART, PT))
    mid_pos = jnp.take_along_axis(middle, mid_rank ^ 1, axis=1)
    centre = parts * PT + HALO_T + mid_pos
    result = jnp.where(pos[None, :] >= PT - HALO_T, upper, jnp.where(pos[None, :] < HALO_T, lower, centre))
    return result.reshape(NT).astype(jnp.int32)


def build_graph(key):
    pair_key = jax.random.fold_in(key, 1)
    value_key = jax.random.fold_in(key, 2)
    live_key = jax.random.fold_in(key, 3)
    rows = jnp.arange(NT, dtype=jnp.int32)
    all_vals = []
    all_cols = []
    all_live = []
    for slot in range(K):
        round_key = jax.random.fold_in(pair_key, slot)
        if slot % 4 == 0:
            partner = cross_partners(round_key)
        else:
            partner = intra_partners(round_key)
        low = jnp.minimum(rows, partner)

        def one_tile(row, col, lowest):
            tile_key = jax.random.fold_in(jax.random.fold_in(value_key, slot), lowest)
            values = jax.random.uniform(jax.random.fold_in(tile_key, 1), (128, 128), jnp.float32, 0.5, 1.5)
            present = jax.random.randint(jax.random.fold_in(tile_key, 2), (128, 128), 0, 2).astype(jnp.float32)
            block = values * present
            return jnp.where(row < col, block, jnp.where(row > col, block.T, block + block.T))

        def one_live(lowest):
            draw_key = jax.random.fold_in(jax.random.fold_in(live_key, slot), lowest)
            level = jax.random.randint(draw_key, (), 0, 4)
            return (level < lowest // PT % 4 + 1).astype(jnp.int32)
        all_vals.append(jax.vmap(one_tile)(rows, partner, low))
        all_cols.append(partner)
        all_live.append(jax.vmap(one_live)(low))
    return (jnp.stack(all_vals, axis=1), jnp.stack(all_cols, axis=1), jnp.stack(all_live, axis=1))


def draw_tile_vals(key, part):
    return build_graph(jax.random.fold_in(key, 7))[0].astype(jnp.bfloat16)


def draw_tile_cols(key, part):
    return build_graph(jax.random.fold_in(key, 7))[1].astype(jnp.int32)


def draw_tile_live(key, part):
    return build_graph(jax.random.fold_in(key, 7))[2].astype(jnp.int32)


def block_levels(stream_key, dims, cuts, least, high):
    gain = 1.0
    for axis_at, shards_of in cuts:
        steps = jax.random.uniform(jax.random.fold_in(jax.random.fold_in(stream_key, 6), axis_at), (shards_of,), jnp.float32, least / len(cuts), high / len(cuts))
        gain = gain * jnp.repeat(jnp.exp(steps), dims[axis_at] // shards_of).reshape((-1,) + (1,) * (len(dims) - 1 - axis_at))
    return gain


def bell_draw(key, extent, spread, most, pieces=(), kind=jnp.bfloat16):
    drawn = spread * jax.random.normal(key, extent, jnp.float32)
    if pieces:
        drawn = drawn * block_levels(key, extent, pieces, -0.22, 0.18)
    return jnp.clip(drawn, -most, most).astype(kind)


def setup_inputs(seed: int = 0) -> dict:
    key_list = jax.random.split(jax.random.key(seed), 10)
    return {
        "x_loader": bell_draw(key_list[0], (V, F), 1.0, 6.0, ((0, 32),)),
        "owner_index": draw_owner_index(jax.random.fold_in(key_list[9], 71), 0),
        "tile_vals": draw_tile_vals(jax.random.fold_in(key_list[9], 71), 0),
        "tile_cols": draw_tile_cols(jax.random.fold_in(key_list[9], 71), 0),
        "tile_live": draw_tile_live(jax.random.fold_in(key_list[9], 71), 0),
        "w_self": bell_draw(key_list[5], (F, F), F ** -0.5, 0.25),
        "w_neigh": bell_draw(key_list[6], (F, F), 0.5, 3.0),
        "bias": bell_draw(key_list[7], (F,), 0.5, 3.0, (), jnp.float32),
        "cotangent": bell_draw(key_list[8], (V, F), 1.0, 6.0, ((0, 32),)),
    }


def reference(x_loader, owner_index, tile_vals, tile_cols, tile_live, w_self, w_neigh, bias, cotangent):
    total, width = x_loader.shape
    tiles = tile_vals.shape[0]
    slots = tile_vals.shape[1]
    groups = tiles // 8
    features = jnp.zeros((total, width), jnp.bfloat16).at[owner_index].set(x_loader)
    masked = tile_vals * tile_live.astype(jnp.bfloat16)[:, :, None, None]
    degree = 1.0 + jnp.sum(masked.astype(jnp.float32), axis=(1, 3))
    blocks_all = features.reshape(tiles, 128, width)
    masked_groups = masked.reshape(groups, 8, slots, 128, 128)
    col_groups = tile_cols.reshape(groups, 8, slots)

    def forward_group(args):
        vals, cols = args
        picked = blocks_all[cols].astype(jnp.float32)
        return jnp.einsum("gkab,gkbf->gaf", vals.astype(jnp.float32), picked)

    summed = lax.map(forward_group, (masked_groups, col_groups)).reshape(total, width)
    agg = (summed / degree.reshape(total, 1)).astype(jnp.bfloat16)
    pre = jnp.dot(features, w_self, preferred_element_type=jnp.float32) + jnp.dot(agg, w_neigh, preferred_element_type=jnp.float32) + bias.astype(jnp.float32)
    layer_out = jnp.where(pre > 0, pre, jnp.expm1(jnp.minimum(pre, 0.0))).astype(jnp.bfloat16)
    slope = jnp.where(pre > 0, 1.0, jnp.exp(jnp.minimum(pre, 0.0)))
    dz = (cotangent.astype(jnp.float32) * slope).astype(jnp.bfloat16)
    grad_self = jnp.dot(features.T, dz, preferred_element_type=jnp.float32)
    grad_neigh = jnp.dot(agg.T, dz, preferred_element_type=jnp.float32)
    grad_bias = jnp.sum(dz.astype(jnp.float32), axis=0)
    scaled = (jnp.dot(dz, w_neigh.T, preferred_element_type=jnp.float32) / degree.reshape(total, 1)).astype(jnp.bfloat16)
    scaled_groups = scaled.reshape(groups, 8, 128, width)

    def backward_group(carry, args):
        vals, cols, rows = args
        terms = jnp.einsum("gkab,gaf->gkbf", vals.astype(jnp.float32), rows.astype(jnp.float32))
        carry = carry.at[cols.reshape(-1)].add(terms.reshape(-1, 128, width))
        return carry, None

    start = jnp.zeros((tiles, 128, width), jnp.float32)
    back, _ = lax.scan(backward_group, start, (masked_groups, col_groups, scaled_groups))
    grad_features = (jnp.dot(dz, w_self.T, preferred_element_type=jnp.float32) + back.reshape(total, width)).astype(jnp.bfloat16)
    return layer_out, grad_features, grad_self, grad_neigh, grad_bias
```

```python
import functools

import jax
import jax.numpy as jnp
from jax import lax
from jax.experimental import pallas as pl
from jax.experimental.pallas import tpu as pltpu
from jax.sharding import PartitionSpec as P

HALO_T = 4
LANES = 128
PIECES = 2
MESH = pl.DeviceIdType.MESH
F32 = jnp.float32
BF16 = jnp.bfloat16


def dot(a, b):
    return jnp.dot(a, b, preferred_element_type=F32)


def dot_rows(a, b):
    return lax.dot_general(a, b, (((0,), (0,)), ((), ())), preferred_element_type=F32)


def dot_cols(a, b):
    return lax.dot_general(a, b, (((1,), (1,)), ((), ())), preferred_element_type=F32)


def kernel(
    parts, reps,
    x_ref, owner_ref, vals_ref, cols_ref, live_ref, ws_ref, wn_ref, bias_ref, cot_ref,
    out_ref, gf_ref, gs_ref, gn_ref, gb_ref,
    mv_send, mv_recv, sl_send, sl_recv, fa, ext_f, ext_s, wm, deg, dz, brow,
    a_send, a_recv, b_send, b_recv, fin, bias_a, bias_b,
    mv_ss, mv_rs, sl_ss, sl_rs, e_ss, e_rs,
    a_ss, a_rs, b_ss, b_rs, gb_ss, gb_rs, ga_ss, ga_rs, ba_ss, ba_rs, bb_ss, bb_rs,
):
    p = lax.axis_index("dom")
    r = lax.axis_index("rep")
    rows, width = x_ref.shape
    tiles = rows // LANES
    slots = vals_ref.shape[1]
    share = rows // parts
    piece = tiles // PIECES
    r1 = r + 1 - 2 * lax.rem(r, 2)
    r2 = lax.rem(r + 2, 4)
    r3 = 3 - r

    def remote(src, dst, ss, rs, dom, rep):
        return pltpu.make_async_remote_copy(
            src_ref=src, dst_ref=dst, send_sem=ss, recv_sem=rs,
            device_id=(dom, rep), device_id_type=MESH,
        )

    barrier = pltpu.get_barrier_semaphore()
    for i in range(1, reps):
        pl.semaphore_signal(barrier, inc=1, device_id=(p, lax.rem(r + i, reps)), device_id_type=MESH)
    for i in range(1, parts):
        pl.semaphore_signal(barrier, inc=1, device_id=(lax.rem(p + i, parts), r), device_id_type=MESH)

    owner = owner_ref[...]
    dest = lax.div(owner, rows * reps)
    slot = lax.rem(owner, rows)
    kinds = max(parts, 16)
    hot = lax.broadcasted_iota(jnp.int32, (kinds, rows), 0) == dest
    before = (
        lax.broadcasted_iota(jnp.int32, (rows, rows), 0)
        < lax.broadcasted_iota(jnp.int32, (rows, rows), 1)
    ).astype(F32).astype(BF16)
    counts = dot(hot.astype(F32).astype(BF16), before)
    rank = jnp.sum(jnp.where(hot, counts, 0.0), axis=0, keepdims=True)
    pos = dest * share + rank.astype(jnp.int32)
    pick = lax.broadcasted_iota(jnp.int32, (rows, rows), 0) == pos
    moved = dot(pick.astype(F32).astype(BF16), x_ref[...]).astype(BF16)
    where_to = jnp.sum(jnp.where(pick, slot.astype(F32), 0.0), axis=1, keepdims=True)
    mv_send[...] = moved.reshape(parts, share, width)
    sl_send[...] = jnp.broadcast_to(where_to.astype(jnp.int32), (rows, LANES)).reshape(parts, share, LANES)

    pl.semaphore_wait(barrier, reps - 1 + parts - 1)

    def to_parts(src, dst, ss, rs, i):
        peer = lax.rem(p + i, parts)
        return remote(src(peer), dst(p), ss.at[i], rs.at[p], peer, r)

    def from_parts(src, dst, ss, rs, i):
        peer = lax.rem(p + parts - i, parts)
        return remote(src(peer), dst(peer), ss.at[i], rs.at[peer], peer, r)

    def to_reps(src, dst, ss, rs, i):
        peer = lax.rem(r + i, reps)
        return remote(src(peer), dst(r), ss.at[i], rs.at[r], p, peer)

    def from_reps(src, dst, ss, rs, i):
        peer = lax.rem(r + reps - i, reps)
        return remote(src(peer), dst(peer), ss.at[i], rs.at[peer], p, peer)

    def at(ref):
        return lambda k: ref.at[k]

    sl = (at(sl_send), at(sl_recv), sl_ss, sl_rs)
    mv = (at(mv_send), at(mv_recv), mv_ss, mv_rs)
    for i in range(1, parts):
        to_parts(*mv, i).start()
        to_parts(*sl, i).start()
    mv_recv[p] = mv_send[p]
    sl_recv[p] = sl_send[p]

    def mask_tiles(t, carry):
        total = jnp.zeros((LANES, LANES), F32)
        for k in range(slots):
            tile = vals_ref[t, k].astype(F32) * live_ref[t, k].astype(F32)
            total = total + tile
            wm[t, :, k * LANES:(k + 1) * LANES] = tile.astype(BF16)
        degree = 1.0 + jnp.sum(total, axis=1, keepdims=True)
        deg[t] = jnp.broadcast_to(degree, (LANES, LANES))
        return carry

    lax.fori_loop(0, tiles, mask_tiles, 0)

    for i in range(1, parts):
        from_parts(*mv, i).wait_recv()
        from_parts(*sl, i).wait_recv()
    landed = sl_recv[...].reshape(rows, LANES)
    place = jnp.concatenate(
        [
            (landed == lax.broadcasted_iota(jnp.int32, (rows, LANES), 1) + c * LANES).astype(F32).astype(BF16)
            for c in range(rows // LANES)
        ],
        axis=1,
    )
    features = dot_rows(place, mv_recv[...].reshape(rows, width)).astype(BF16)
    fa[0] = features
    first = HALO_T + r * tiles
    ext_f[pl.ds(first, tiles)] = features.reshape(tiles, LANES, width)

    def spread(ext, use):
        high = HALO_T + reps * tiles

        def copy(base, c, send, recv, dom, rep, target=None):
            src = ext.at[pl.ds(base + c * piece, piece)]
            dst = src if target is None else ext.at[pl.ds(target + c * piece, piece)]
            return remote(src, dst, e_ss.at[use, send, c], e_rs.at[use, recv, c], dom, rep)

        def block(q):
            return HALO_T + q * tiles

        root_low, root_high = r == reps - 1, r == 0
        more, less = p < parts - 1, p > 0

        def begin():
            for c in range(PIECES):
                copy(block(r), c, 0, 0, p, r2).start()

                @pl.when(jnp.logical_and(root_low, more))
                def _():
                    copy(block(r), c, 3, 3, p + 1, r, 0).start()

                @pl.when(jnp.logical_and(root_high, less))
                def _():
                    copy(block(r), c, 4, 4, p - 1, r, high).start()

                copy(block(r), c, 1, 1, p, r1).start()

        def rim(base, c, recv, send, root, second, there):
            @pl.when(there)
            def _():
                copy(base, c, send, recv, p, r1).wait_recv()

                @pl.when(root)
                def _():
                    copy(base, c, send + 1, recv, p, r2).start()
                    copy(base, c, send, recv, p, r1).start()

                @pl.when(second)
                def _():
                    copy(base, c, send, recv, p, r1).start()

        def forward():
            for c in range(PIECES):
                copy(block(r2), c, 0, 0, p, r2).wait_recv()
                copy(block(r2), c, 2, 2, p, r1).start()
                rim(0, c, 3, 5, root_low, r == 1, less)
                rim(high, c, 4, 7, root_high, r == 2, more)

        def end():
            for c in range(PIECES):
                copy(block(r1), c, 1, 1, p, r1).wait_recv()
                copy(block(r3), c, 2, 2, p, r1).wait_recv()

        def sent():
            for c in range(PIECES):
                copy(block(r), c, 0, 0, p, r2).wait_send()
                copy(block(r), c, 1, 1, p, r1).wait_send()
                copy(block(r2), c, 2, 2, p, r1).wait_send()

                @pl.when(jnp.logical_and(root_low, more))
                def _():
                    copy(block(r), c, 3, 3, p + 1, r, 0).wait_send()

                @pl.when(jnp.logical_and(root_high, less))
                def _():
                    copy(block(r), c, 4, 4, p - 1, r, high).wait_send()

                for base, recv, send, root, second, there in (
                    (0, 3, 5, root_low, r == 1, less),
                    (high, 4, 7, root_high, r == 2, more),
                ):
                    @pl.when(jnp.logical_and(there, root))
                    def _():
                        copy(base, c, send + 1, recv, p, r2).wait_send()
                        copy(base, c, send, recv, p, r1).wait_send()

                    @pl.when(jnp.logical_and(there, second))
                    def _():
                        copy(base, c, send, recv, p, r1).wait_send()

        return begin, forward, end, sent

    begin_f, forward_f, end_f, sent_f = spread(ext_f, 0)
    begin_s, forward_s, end_s, sent_s = spread(ext_s, 1)
    first_tile = p * (reps * tiles) - HALO_T

    def gather(ext, t):
        last = ext.shape[0] - 1
        picked = [ext[jnp.clip(cols_ref[t, k] - first_tile, 0, last)] for k in range(slots)]
        return jnp.concatenate(picked, axis=0)

    begin_f()
    forward_f()
    end_f()

    brow[...] = jnp.zeros(brow.shape, F32)

    def layer(t, carry):
        here = pl.ds(pl.multiple_of(t * LANES, LANES), LANES)
        degree = deg[t][:, 0:1]
        agg = (dot(wm[t], gather(ext_f, t)) / degree).astype(BF16)
        fa[1, here] = agg
        pre = dot(fa[0, here], ws_ref[...]) + dot(agg, wn_ref[...]) + bias_ref[...]
        decay = jnp.exp(jnp.minimum(pre, 0.0))
        out_ref[here] = jnp.where(pre > 0, pre, decay - 1.0).astype(BF16)
        slope = jnp.where(pre > 0, 1.0, decay)
        grad = (cot_ref[here].astype(F32) * slope).astype(BF16)
        dz[here] = grad
        brow[...] += jnp.broadcast_to(jnp.sum(grad.astype(F32), axis=0, keepdims=True), brow.shape)
        ext_s[first + t] = (dot_cols(grad, wn_ref[...]) / degree).astype(BF16)
        return carry

    lax.fori_loop(0, tiles, layer, 0)
    begin_s()

    quarter = 2 * width // reps
    per = reps // 2

    def weight(q, carry):
        column = pl.multiple_of(lax.rem(q, per) * quarter, quarter)
        a_send[q] = dot_rows(fa[lax.div(q, per), :, pl.ds(column, quarter)], dz[...]).astype(BF16)
        return carry

    lax.fori_loop(0, reps, weight, 0)
    bias_a[r] = brow[...]
    a = (at(a_send), at(a_recv), a_ss, a_rs)
    ba = (lambda k: bias_a.at[r], at(bias_a), ba_ss, ba_rs)
    for i in range(1, reps):
        to_reps(*a, i).start()
        to_reps(*ba, i).start()
    a_recv[r] = a_send[r]
    forward_s()

    for i in range(1, reps):
        from_reps(*a, i).wait_recv()
        from_reps(*ba, i).wait_recv()
    high_c, wide_c = b_send.shape[1:]
    across = width // wide_c
    for d in range(parts):
        down, side = d // across * high_c, d % across * wide_c
        total = jnp.zeros((high_c, wide_c), F32)
        for q in range(reps):
            total = total + a_recv[q, down:down + high_c, side:side + wide_c].astype(F32)
        b_send[d] = total.astype(BF16)
    total = bias_a[0]
    for q in range(1, reps):
        total = total + bias_a[q]
    bias_b[p] = total
    b = (at(b_send), at(b_recv), b_ss, b_rs)
    bb = (lambda k: bias_b.at[p], at(bias_b), bb_ss, bb_rs)
    for i in range(1, parts):
        to_parts(*b, i).start()
        to_parts(*bb, i).start()
    b_recv[p] = b_send[p]
    end_s()

    for i in range(1, parts):
        from_parts(*b, i).wait_recv()
        from_parts(*bb, i).wait_recv()
    total = b_recv[0].astype(F32)
    bias_total = bias_b[0]
    for d in range(1, parts):
        total = total + b_recv[d].astype(F32)
        bias_total = bias_total + bias_b[d]
    fin[r, p] = total.astype(BF16)
    gb_ref[...] = bias_total[0:1]
    gb = (lambda k: fin.at[r, p], lambda k: fin.at[r, k], gb_ss, gb_rs)
    for i in range(1, parts):
        to_parts(*gb, i).start()

    def back(t, carry):
        here = pl.ds(pl.multiple_of(t * LANES, LANES), LANES)
        gf_ref[here] = (
            dot_cols(dz[here], ws_ref[...]) + dot(wm[t], gather(ext_s, t))
        ).astype(BF16)
        return carry

    lax.fori_loop(0, tiles, back, 0)

    for i in range(1, parts):
        from_parts(*gb, i).wait_recv()
    ga = (lambda k: fin.at[r], at(fin), ga_ss, ga_rs)
    for i in range(1, reps):
        to_reps(*ga, i).start()
    for i in range(1, reps):
        from_reps(*ga, i).wait_recv()
    for q in range(reps):
        ref = gs_ref if q < per else gn_ref
        for d in range(parts):
            down, side = q % per * quarter + d // across * high_c, d % across * wide_c
            ref[down:down + high_c, side:side + wide_c] = fin[q, d].astype(F32)

    for i in range(1, parts):
        for kind in (mv, sl, b, bb, gb):
            to_parts(*kind, i).wait_send()
    for i in range(1, reps):
        for kind in (a, ba, ga):
            to_reps(*kind, i).wait_send()
    sent_f()
    sent_s()


def shards(
    parts, reps,
    x_loader, owner_index, tile_vals, tile_cols, tile_live, w_self, w_neigh, bias, cotangent
):
    rows, width = x_loader.shape
    tiles, slots = tile_cols.shape
    share = rows // parts
    quarter = 2 * width // reps
    high_c = max(16, quarter // parts)
    wide_c = quarter * width // parts // high_c
    span = reps * tiles + 2 * HALO_T
    dma = pltpu.SemaphoreType.DMA
    vmem = pl.BlockSpec(memory_space=pltpu.VMEM)
    smem = pl.BlockSpec(memory_space=pltpu.SMEM)
    out = pl.pallas_call(
        functools.partial(kernel, parts, reps),
        out_shape=(
            jax.ShapeDtypeStruct((rows, width), BF16),
            jax.ShapeDtypeStruct((rows, width), BF16),
            jax.ShapeDtypeStruct((width, width), F32),
            jax.ShapeDtypeStruct((width, width), F32),
            jax.ShapeDtypeStruct((1, width), F32),
        ),
        in_specs=[vmem, vmem, vmem, smem, smem, vmem, vmem, vmem, vmem],
        out_specs=(vmem,) * 5,
        scratch_shapes=[
            pltpu.VMEM((parts, share, width), BF16),
            pltpu.VMEM((parts, share, width), BF16),
            pltpu.VMEM((parts, share, LANES), jnp.int32),
            pltpu.VMEM((parts, share, LANES), jnp.int32),
            pltpu.VMEM((2, rows, width), BF16),
            pltpu.VMEM((span, LANES, width), BF16),
            pltpu.VMEM((span, LANES, width), BF16),
            pltpu.VMEM((tiles, LANES, slots * LANES), BF16),
            pltpu.VMEM((tiles, LANES, LANES), F32),
            pltpu.VMEM((rows, width), BF16),
            pltpu.VMEM((8, width), F32),
            pltpu.VMEM((reps, quarter, width), BF16),
            pltpu.VMEM((reps, quarter, width), BF16),
            pltpu.VMEM((parts, high_c, wide_c), BF16),
            pltpu.VMEM((parts, high_c, wide_c), BF16),
            pltpu.VMEM((reps, parts, high_c, wide_c), BF16),
            pltpu.VMEM((reps, 8, width), F32),
            pltpu.VMEM((parts, 8, width), F32),
            dma((parts,)), dma((parts,)), dma((parts,)), dma((parts,)),
            dma((2, 9, PIECES)), dma((2, 5, PIECES)),
            dma((reps,)), dma((reps,)), dma((parts,)), dma((parts,)),
            dma((parts,)), dma((parts,)), dma((reps,)), dma((reps,)),
            dma((reps,)), dma((reps,)), dma((parts,)), dma((parts,)),
        ],
        compiler_params=pltpu.CompilerParams(
            collective_id=0, has_side_effects=True, vmem_limit_bytes=48 * 1024 * 1024
        ),
    )(
        x_loader, owner_index.reshape(1, rows), tile_vals, tile_cols, tile_live,
        w_self, w_neigh, bias.reshape(1, width), cotangent,
    )
    return (*out[:4], out[4].reshape(width))


def solution(mesh):
    sharded = P(("dom", "rep"))
    return jax.shard_map(
        functools.partial(shards, mesh.shape["dom"], mesh.shape["rep"]),
        mesh=mesh,
        in_specs=(sharded,) * 5 + (P(), P(), P(), sharded),
        out_specs=(sharded, sharded, P(), P(), P()),
        check_vma=False,
    )
```

```python
import functools

import jax
import jax.numpy as jnp
from jax import lax
from jax.experimental import pallas as pl
from jax.experimental.pallas import tpu as pltpu
from jax.sharding import PartitionSpec as P

HALO_T = 4
LANES = 128
PIECES = 2
MESH = pl.DeviceIdType.MESH
F32 = jnp.float32
BF16 = jnp.bfloat16


def dot(a, b):
    return jnp.dot(a, b, preferred_element_type=F32)


def dot_rows(a, b):
    return lax.dot_general(a, b, (((0,), (0,)), ((), ())), preferred_element_type=F32)


def dot_cols(a, b):
    return lax.dot_general(a, b, (((1,), (1,)), ((), ())), preferred_element_type=F32)


def kernel(
    parts, reps,
    x_ref, owner_ref, vals_ref, cols_ref, live_ref, ws_ref, wn_ref, bias_ref, cot_ref,
    out_ref, gf_ref, gs_ref, gn_ref, gb_ref,
    mv_send, mv_recv, sl_send, sl_recv, fa, ext_f, ext_s, wm, deg, dz, brow,
    a_send, a_recv, b_send, b_recv, fin, bias_a, bias_b,
    mv_ss, mv_rs, sl_ss, sl_rs, e_ss, e_rs,
    a_ss, a_rs, b_ss, b_rs, gb_ss, gb_rs, ga_ss, ga_rs, ba_ss, ba_rs, bb_ss, bb_rs,
):
    p = lax.axis_index("dom")
    r = lax.axis_index("rep")
    rows, width = x_ref.shape
    tiles = rows // LANES
    slots = vals_ref.shape[1]
    share = rows // parts
    piece = tiles // PIECES
    r1 = r + 1 - 2 * lax.rem(r, 2)
    r2 = lax.rem(r + 2, 4)
    r3 = 3 - r

    def remote(src, dst, ss, rs, dom, rep):
        return pltpu.make_async_remote_copy(
            src_ref=src, dst_ref=dst, send_sem=ss, recv_sem=rs,
            device_id=(dom, rep), device_id_type=MESH,
        )

    barrier = pltpu.get_barrier_semaphore()
    for i in range(1, reps):
        pl.semaphore_signal(barrier, inc=1, device_id=(p, lax.rem(r + i, reps)), device_id_type=MESH)
    for i in range(1, parts):
        pl.semaphore_signal(barrier, inc=1, device_id=(lax.rem(p + i, parts), r), device_id_type=MESH)

    owner = owner_ref[...]
    dest = lax.div(owner, rows * reps)
    slot = lax.rem(owner, rows)
    kinds = max(parts, 16)
    hot = lax.broadcasted_iota(jnp.int32, (kinds, rows), 0) == dest
    before = (
        lax.broadcasted_iota(jnp.int32, (rows, rows), 0)
        < lax.broadcasted_iota(jnp.int32, (rows, rows), 1)
    ).astype(F32).astype(BF16)
    counts = dot(hot.astype(F32).astype(BF16), before)
    rank = jnp.sum(jnp.where(hot, counts, 0.0), axis=0, keepdims=True)
    pos = dest * share + rank.astype(jnp.int32)
    pick = lax.broadcasted_iota(jnp.int32, (rows, rows), 0) == pos
    moved = dot(pick.astype(F32).astype(BF16), x_ref[...]).astype(BF16)
    where_to = jnp.sum(jnp.where(pick, slot.astype(F32), 0.0), axis=1, keepdims=True)
    mv_send[...] = moved.reshape(parts, share, width)
    sl_send[...] = jnp.broadcast_to(where_to.astype(jnp.int32), (rows, LANES)).reshape(parts, share, LANES)

    pl.semaphore_wait(barrier, reps - 1 + parts - 1)

    def to_parts(src, dst, ss, rs, i):
        peer = lax.rem(p + i, parts)
        return remote(src(peer), dst(p), ss.at[i], rs.at[p], peer, r)

    def from_parts(src, dst, ss, rs, i):
        peer = lax.rem(p + parts - i, parts)
        return remote(src(peer), dst(peer), ss.at[i], rs.at[peer], peer, r)

    def to_reps(src, dst, ss, rs, i):
        peer = lax.rem(r + i, reps)
        return remote(src(peer), dst(r), ss.at[i], rs.at[r], p, peer)

    def from_reps(src, dst, ss, rs, i):
        peer = lax.rem(r + reps - i, reps)
        return remote(src(peer), dst(peer), ss.at[i], rs.at[peer], p, peer)

    def at(ref):
        return lambda k: ref.at[k]

    sl = (at(sl_send), at(sl_recv), sl_ss, sl_rs)
    mv = (at(mv_send), at(mv_recv), mv_ss, mv_rs)
    for i in range(1, parts):
        to_parts(*mv, i).start()
        to_parts(*sl, i).start()
    mv_recv[p] = mv_send[p]
    sl_recv[p] = sl_send[p]

    def mask_tiles(t, carry):
        total = jnp.zeros((LANES, LANES), F32)
        for k in range(slots):
            tile = vals_ref[t, k].astype(F32) * live_ref[t, k].astype(F32)
            total = total + tile
            wm[t, :, k * LANES:(k + 1) * LANES] = tile.astype(BF16)
        degree = 1.0 + jnp.sum(total, axis=1, keepdims=True)
        deg[t] = jnp.broadcast_to(degree, (LANES, LANES))
        return carry

    lax.fori_loop(0, tiles, mask_tiles, 0)

    for i in range(1, parts):
        from_parts(*mv, i).wait_recv()
        from_parts(*sl, i).wait_recv()
    landed = sl_recv[...].reshape(rows, LANES)
    place = jnp.concatenate(
        [
            (landed == lax.broadcasted_iota(jnp.int32, (rows, LANES), 1) + c * LANES).astype(F32).astype(BF16)
            for c in range(rows // LANES)
        ],
        axis=1,
    )
    features = dot_rows(place, mv_recv[...].reshape(rows, width)).astype(BF16)
    fa[0] = features
    first = HALO_T + r * tiles
    ext_f[pl.ds(first, tiles)] = features.reshape(tiles, LANES, width)

    def spread(ext, use):
        high = HALO_T + reps * tiles

        def copy(base, c, send, recv, dom, rep, target=None):
            src = ext.at[pl.ds(base + c * piece, piece)]
            dst = src if target is None else ext.at[pl.ds(target + c * piece, piece)]
            return remote(src, dst, e_ss.at[use, send, c], e_rs.at[use, recv, c], dom, rep)

        def block(q):
            return HALO_T + q * tiles

        root_low, root_high = r == reps - 1, r == 0
        more, less = p < parts - 1, p > 0

        def begin():
            for c in range(PIECES):
                copy(block(r), c, 0, 0, p, r2).start()

                @pl.when(jnp.logical_and(root_low, more))
                def _():
                    copy(block(r), c, 3, 3, p + 1, r, 0).start()

                @pl.when(jnp.logical_and(root_high, less))
                def _():
                    copy(block(r), c, 4, 4, p - 1, r, high).start()

                copy(block(r), c, 1, 1, p, r1).start()

        def rim(base, c, recv, send, root, second, there):
            @pl.when(there)
            def _():
                copy(base, c, send, recv, p, r1).wait_recv()

                @pl.when(root)
                def _():
                    copy(base, c, send + 1, recv, p, r2).start()
                    copy(base, c, send, recv, p, r1).start()

                @pl.when(second)
                def _():
                    copy(base, c, send, recv, p, r1).start()

        def forward():
            for c in range(PIECES):
                copy(block(r2), c, 0, 0, p, r2).wait_recv()
                copy(block(r2), c, 2, 2, p, r1).start()
                rim(0, c, 3, 5, root_low, r == 1, less)
                rim(high, c, 4, 7, root_high, r == 2, more)

        def end():
            for c in range(PIECES):
                copy(block(r1), c, 1, 1, p, r1).wait_recv()
                copy(block(r3), c, 2, 2, p, r1).wait_recv()

        def sent():
            for c in range(PIECES):
                copy(block(r), c, 0, 0, p, r2).wait_send()
                copy(block(r), c, 1, 1, p, r1).wait_send()
                copy(block(r2), c, 2, 2, p, r1).wait_send()

                @pl.when(jnp.logical_and(root_low, more))
                def _():
                    copy(block(r), c, 3, 3, p + 1, r, 0).wait_send()

                @pl.when(jnp.logical_and(root_high, less))
                def _():
                    copy(block(r), c, 4, 4, p - 1, r, high).wait_send()

                for base, recv, send, root, second, there in (
                    (0, 3, 5, root_low, r == 1, less),
                    (high, 4, 7, root_high, r == 2, more),
                ):
                    @pl.when(jnp.logical_and(there, root))
                    def _():
                        copy(base, c, send + 1, recv, p, r2).wait_send()
                        copy(base, c, send, recv, p, r1).wait_send()

                    @pl.when(jnp.logical_and(there, second))
                    def _():
                        copy(base, c, send, recv, p, r1).wait_send()

        return begin, forward, end, sent

    begin_f, forward_f, end_f, sent_f = spread(ext_f, 0)
    begin_s, forward_s, end_s, sent_s = spread(ext_s, 1)
    first_tile = p * (reps * tiles) - HALO_T

    def gather(ext, t):
        last = ext.shape[0] - 1
        picked = [ext[jnp.clip(cols_ref[t, k] - first_tile, 0, last)] for k in range(slots)]
        return jnp.concatenate(picked, axis=0)

    begin_f()
    forward_f()
    end_f()

    brow[...] = jnp.zeros(brow.shape, F32)

    def layer(t, carry):
        here = pl.ds(pl.multiple_of(t * LANES, LANES), LANES)
        degree = deg[t][:, 0:1]
        agg = (dot(wm[t], gather(ext_f, t)) / degree).astype(BF16)
        fa[1, here] = agg
        pre = dot(fa[0, here], ws_ref[...]) + dot(agg, wn_ref[...]) + bias_ref[...]
        decay = jnp.exp(jnp.minimum(pre, 0.0))
        out_ref[here] = jnp.where(pre > 0, pre, decay - 1.0).astype(BF16)
        slope = jnp.where(pre > 0, 1.0, decay)
        grad = (cot_ref[here].astype(F32) * slope).astype(BF16)
        dz[here] = grad
        brow[...] += jnp.broadcast_to(jnp.sum(grad.astype(F32), axis=0, keepdims=True), brow.shape)
        ext_s[first + t] = (dot_cols(grad, wn_ref[...]) / degree).astype(BF16)
        return carry

    lax.fori_loop(0, tiles, layer, 0)
    begin_s()

    quarter = 2 * width // reps
    per = reps // 2

    def weight(q, carry):
        column = pl.multiple_of(lax.rem(q, per) * quarter, quarter)
        a_send[q] = dot_rows(fa[lax.div(q, per), :, pl.ds(column, quarter)], dz[...]).astype(BF16)
        return carry

    lax.fori_loop(0, reps, weight, 0)
    bias_a[r] = brow[...]

    def a_copy(src, k, peer):
        return remote(src, a_recv.at[k], a_ss.at[k], a_rs.at[k], p, peer)

    cross = a_copy(a_send.at[r3], 1, r1)
    near = a_copy(a_send.at[r1], 0, r1)
    far = a_copy(a_recv.at[3], 2, r2)
    cross.start()
    near.start()
    ba = (lambda k: bias_a.at[r], at(bias_a), ba_ss, ba_rs)
    for i in range(1, reps):
        to_reps(*ba, i).start()
    cross.wait_recv()
    a_recv[3] = (a_send[r2].astype(F32) + a_recv[1].astype(F32)).astype(BF16)
    far.start()
    forward_s()

    for i in range(1, reps):
        from_reps(*ba, i).wait_recv()
    near.wait_recv()
    far.wait_recv()
    high_c, wide_c = b_send.shape[1:]
    across = width // wide_c
    for d in range(parts):
        down, side = d // across * high_c, d % across * wide_c
        total = a_send[r, down:down + high_c, side:side + wide_c].astype(F32)
        for q in (0, 2):
            total = total + a_recv[q, down:down + high_c, side:side + wide_c].astype(F32)
        b_send[d] = total.astype(BF16)
    total = bias_a[0]
    for q in range(1, reps):
        total = total + bias_a[q]
    bias_b[p] = total
    b = (at(b_send), at(b_recv), b_ss, b_rs)
    bb = (lambda k: bias_b.at[p], at(bias_b), bb_ss, bb_rs)
    for i in range(1, parts):
        to_parts(*b, i).start()
        to_parts(*bb, i).start()
    b_recv[p] = b_send[p]
    end_s()

    for i in range(1, parts):
        from_parts(*b, i).wait_recv()
        from_parts(*bb, i).wait_recv()
    total = b_recv[0].astype(F32)
    bias_total = bias_b[0]
    for d in range(1, parts):
        total = total + b_recv[d].astype(F32)
        bias_total = bias_total + bias_b[d]
    fin[r, p] = total.astype(BF16)
    gb_ref[...] = bias_total[0:1]
    gb = (lambda k: fin.at[r, p], lambda k: fin.at[r, k], gb_ss, gb_rs)
    for i in range(1, parts):
        to_parts(*gb, i).start()

    def back(t, carry):
        here = pl.ds(pl.multiple_of(t * LANES, LANES), LANES)
        gf_ref[here] = (
            dot_cols(dz[here], ws_ref[...]) + dot(wm[t], gather(ext_s, t))
        ).astype(BF16)
        return carry

    lax.fori_loop(0, tiles, back, 0)

    for i in range(1, parts):
        from_parts(*gb, i).wait_recv()

    def g_copy(k, send, peer):
        return remote(fin.at[k], fin.at[k], ga_ss.at[send], ga_rs.at[k], p, peer)

    g_copy(r, 0, r2).start()
    g_copy(r, 1, r1).start()
    g_copy(r2, 0, r2).wait_recv()
    g_copy(r2, 2, r1).start()
    g_copy(r1, 1, r1).wait_recv()
    g_copy(r3, 2, r1).wait_recv()
    for q in range(reps):
        ref = gs_ref if q < per else gn_ref
        for d in range(parts):
            down, side = q % per * quarter + d // across * high_c, d % across * wide_c
            ref[down:down + high_c, side:side + wide_c] = fin[q, d].astype(F32)

    for i in range(1, parts):
        for kind in (mv, sl, b, bb, gb):
            to_parts(*kind, i).wait_send()
    for i in range(1, reps):
        to_reps(*ba, i).wait_send()
    for copy in (cross, near, far, g_copy(r, 0, r2), g_copy(r, 1, r1), g_copy(r2, 2, r1)):
        copy.wait_send()
    sent_f()
    sent_s()


def shards(
    parts, reps,
    x_loader, owner_index, tile_vals, tile_cols, tile_live, w_self, w_neigh, bias, cotangent
):
    rows, width = x_loader.shape
    tiles, slots = tile_cols.shape
    share = rows // parts
    quarter = 2 * width // reps
    high_c = max(16, quarter // parts)
    wide_c = quarter * width // parts // high_c
    span = reps * tiles + 2 * HALO_T
    dma = pltpu.SemaphoreType.DMA
    vmem = pl.BlockSpec(memory_space=pltpu.VMEM)
    smem = pl.BlockSpec(memory_space=pltpu.SMEM)
    out = pl.pallas_call(
        functools.partial(kernel, parts, reps),
        out_shape=(
            jax.ShapeDtypeStruct((rows, width), BF16),
            jax.ShapeDtypeStruct((rows, width), BF16),
            jax.ShapeDtypeStruct((width, width), F32),
            jax.ShapeDtypeStruct((width, width), F32),
            jax.ShapeDtypeStruct((1, width), F32),
        ),
        in_specs=[vmem, vmem, vmem, smem, smem, vmem, vmem, vmem, vmem],
        out_specs=(vmem,) * 5,
        scratch_shapes=[
            pltpu.VMEM((parts, share, width), BF16),
            pltpu.VMEM((parts, share, width), BF16),
            pltpu.VMEM((parts, share, LANES), jnp.int32),
            pltpu.VMEM((parts, share, LANES), jnp.int32),
            pltpu.VMEM((2, rows, width), BF16),
            pltpu.VMEM((span, LANES, width), BF16),
            pltpu.VMEM((span, LANES, width), BF16),
            pltpu.VMEM((tiles, LANES, slots * LANES), BF16),
            pltpu.VMEM((tiles, LANES, LANES), F32),
            pltpu.VMEM((rows, width), BF16),
            pltpu.VMEM((8, width), F32),
            pltpu.VMEM((reps, quarter, width), BF16),
            pltpu.VMEM((reps, quarter, width), BF16),
            pltpu.VMEM((parts, high_c, wide_c), BF16),
            pltpu.VMEM((parts, high_c, wide_c), BF16),
            pltpu.VMEM((reps, parts, high_c, wide_c), BF16),
            pltpu.VMEM((reps, 8, width), F32),
            pltpu.VMEM((parts, 8, width), F32),
            dma((parts,)), dma((parts,)), dma((parts,)), dma((parts,)),
            dma((2, 9, PIECES)), dma((2, 5, PIECES)),
            dma((reps,)), dma((reps,)), dma((parts,)), dma((parts,)),
            dma((parts,)), dma((parts,)), dma((reps,)), dma((reps,)),
            dma((reps,)), dma((reps,)), dma((parts,)), dma((parts,)),
        ],
        compiler_params=pltpu.CompilerParams(
            collective_id=0, has_side_effects=True, vmem_limit_bytes=48 * 1024 * 1024
        ),
    )(
        x_loader, owner_index.reshape(1, rows), tile_vals, tile_cols, tile_live,
        w_self, w_neigh, bias.reshape(1, width), cotangent,
    )
    return (*out[:4], out[4].reshape(width))


def solution(mesh):
    sharded = P(("dom", "rep"))
    return jax.shard_map(
        functools.partial(shards, mesh.shape["dom"], mesh.shape["rep"]),
        mesh=mesh,
        in_specs=(sharded,) * 5 + (P(), P(), P(), sharded),
        out_specs=(sharded, sharded, P(), P(), P()),
        check_vma=False,
    )
```
